32 devices in a mesh: space: 8 (over y, x, core), band: 4 (over z).
Axes of the slice: x: 2, y: 2, z: 4, core: 2. Of those that a mesh axis runs over, the one named last changes fastest.
Arguments:
- blocks: float32 [2, 32, 32, 6144], P(None, 'band', 'space'), may hold values from -304 to 304
- later: float32 [256, 32, 6144], P('band', 'space'), may hold values from -304 to 304
- potential: float32 [32, 6144], P('space'), may hold values from -1.5 to 1.5
Outputs:
- h_block: float32 [2, 32, 32, 6144], P(None, 'band', 'space')
- h_later: float32 [256, 32, 6144], P('band', 'space')
The draws below stay inside these ranges and needn't reach their ends.
All inputs are finite; a program needn't handle non-finite values.
Results may differ from the reference program's by a relative error of at most 0.00009.
Values sent between devices are 32-bit elements; how exact they have to be, the bound alone decides.
No kernel may reach another device: no remote copies, remote signals or barrier semaphores. Data moves between devices by JAX's collectives and lax.ppermute only.
A program may use at most 128 MiB of HBM per device.

```python
import jax
import jax.numpy as jnp
from jax import lax

NY = 64
NZ = 96
BLOCK = 32
LATER = 256
NX = 32


def shared_fields(key):
    return jax.random.truncated_normal(jax.random.fold_in(key, 7), -4.0, 4.0, (4, NX, NY * NZ), jnp.float32)


def envelope_field():
    xpos = lax.broadcasted_iota(jnp.float32, (NX, 1), 0) / (NX - 1)
    return 0.5 + 1.5 * xpos


def mixed_orbitals(key, count, salt):
    shared = shared_fields(key)
    noise = jax.random.truncated_normal(jax.random.fold_in(key, salt), -4.0, 4.0, (count, NX, NY * NZ), jnp.float32)
    mixing = jax.random.uniform(jax.random.fold_in(key, salt + 1), (count, 4), jnp.float32, -0.7, 0.7)
    total = noise
    for index in range(4):
        total = total + mixing[:, index, None, None] * shared[index][None]
    return total * envelope_field()[None]


def draw_blocks(key, part):
    return mixed_orbitals(key, 2 * BLOCK, 21).reshape(2, BLOCK, NX, NY * NZ)


def draw_later(key, part):
    return mixed_orbitals(key, LATER, 31)


def level_of(stream_key, shape, shards, least, largest):
    factor_of, own = 1.0, jax.random.fold_in(stream_key, 6)
    for dim, parts in shards:
        draws = jnp.exp(jax.random.uniform(jax.random.fold_in(own, dim), (parts,), jnp.float32, least / len(shards), largest / len(shards)))
        factor_of = factor_of * jnp.repeat(draws, shape[dim] // parts).reshape([-1 if axis == dim else 1 for axis in range(len(shape))])
    return factor_of


def setup_inputs(seed: int = 0) -> dict:
    keys = jax.random.split(jax.random.key(seed), 4)
    blocks = draw_blocks(jax.random.fold_in(keys[3], 71), 0)
    later = draw_later(jax.random.fold_in(keys[3], 71), 0)
    potential = jnp.clip(jax.random.uniform(keys[2], (NX, NY * NZ), jnp.float32, -1.5, 1.5) * level_of(keys[2], (NX, NY * NZ), ((0, 8),), -0.4, 0.0), -1.5, 1.5)
    return {"blocks": blocks, "later": later, "potential": potential}


stencil_weights = (-205.0 / 72.0, 8.0 / 5.0, -1.0 / 5.0, 8.0 / 315.0, -1.0 / 560.0)

def stencil(extended, potential, depth):
    center = extended[:, 4:-4]
    planes = center.shape[1]
    length = center.shape[2]
    laplace = 3.0 * stencil_weights[0] * center
    for step in range(1, 5):
        laplace = laplace + stencil_weights[step] * (extended[:, 4 + step:4 + step + planes] + extended[:, 4 - step:4 - step + planes])
    margin = 4 * depth
    ypadded = jnp.pad(center, ((0, 0), (0, 0), (margin, margin)))
    for step in range(1, 5):
        upper = ypadded[:, :, margin + step * depth:margin + step * depth + length]
        lower = ypadded[:, :, margin - step * depth:margin - step * depth + length]
        laplace = laplace + stencil_weights[step] * (upper + lower)
    zpadded = jnp.pad(center, ((0, 0), (0, 0), (4, 4)))
    zpos = lax.broadcasted_iota(jnp.int32, (length,), 0) % depth
    for step in range(1, 5):
        upper = jnp.where(zpos + step < depth, zpadded[:, :, 4 + step:4 + step + length], 0.0)
        lower = jnp.where(zpos - step >= 0, zpadded[:, :, 4 - step:4 - step + length], 0.0)
        laplace = laplace + stencil_weights[step] * (upper + lower)
    return -0.5 * laplace + potential[None] * center

def inner(left, right):
    return jnp.dot(left.astype(jnp.float32), right.T.astype(jnp.float32), precision=lax.Precision.HIGHEST, preferred_element_type=jnp.float32)

def apply_rows(left, right):
    return jnp.dot(left.astype(jnp.float32), right.astype(jnp.float32), precision=lax.Precision.HIGHEST, preferred_element_type=jnp.float32)

def reference(blocks, later, potential):
    cells = NX * NY * NZ
    flat = blocks.reshape(2, BLOCK, cells)
    first = flat[0]
    second = flat[1]
    lower_one = jnp.linalg.cholesky(inner(first, first) / cells)
    q_first = lax.linalg.triangular_solve(lower_one, first, left_side=True, lower=True)
    crossed = inner(q_first, second) / cells
    remainder = second - apply_rows(crossed.T, q_first)
    lower_two = jnp.linalg.cholesky(inner(remainder, remainder) / cells)
    q_second = lax.linalg.triangular_solve(lower_two, remainder, left_side=True, lower=True)
    basis = jnp.concatenate([q_first, q_second], axis=0)
    later_flat = later.reshape(LATER, cells)
    weights = inner(basis, later_flat) / cells
    projected = later_flat - apply_rows(weights.T, basis)
    states = jnp.concatenate([basis, projected], axis=0).reshape((2 * BLOCK + LATER) // BLOCK, BLOCK, NX, NY * NZ)

    def one_group(group):
        extended = jnp.pad(group, ((0, 0), (4, 4), (0, 0)))
        return stencil(extended, potential, NZ)
    applied = lax.map(one_group, states).reshape(2 * BLOCK + LATER, NX, NY * NZ)
    h_block = applied[:2 * BLOCK].reshape(2, BLOCK, NX, NY * NZ)
    h_later = applied[2 * BLOCK:]
    return (h_block, h_later)
```

```python
import jax
import jax.numpy as jnp
import numpy as np
from jax import lax
from jax.experimental import pallas as pl
from jax.experimental.pallas import tpu as pltpu
from jax.sharding import PartitionSpec as P

NZ = 96
REACH = 4

stencil_weights = (-205.0 / 72.0, 8.0 / 5.0, -1.0 / 5.0, 8.0 / 315.0, -1.0 / 560.0)
half_weights = tuple(-0.5 * w for w in stencil_weights)

GROUP = 4 * NZ


def split(x):
    high = x.astype(jnp.bfloat16)
    low = (x - high.astype(jnp.float32)).astype(jnp.bfloat16)
    return high, low


def split_matrix(x):
    high = lax.reduce_precision(x, 8, 7)
    low = lax.reduce_precision(x - high, 8, 7)
    return high.astype(jnp.bfloat16), low.astype(jnp.bfloat16)


def dot(a, b, dims=((1,), (0,))):
    return lax.dot_general(a, b, (dims, ((), ())), preferred_element_type=jnp.float32)


def plane_matrix(offset):
    out = np.zeros((REACH, REACH), np.float32)
    for p in range(REACH):
        for q in range(REACH):
            shift = abs(q + offset - p)
            if 1 <= shift <= REACH:
                out[p, q] = half_weights[shift]
    return out


def yz_matrix():
    a = np.arange(3 * GROUP)[:, None]
    o = np.arange(GROUP)[None, :] + GROUP
    dy = np.abs(a // NZ - o // NZ)
    dz = np.abs(a % NZ - o % NZ)
    out = np.zeros((3 * GROUP, GROUP), np.float64)
    for step in range(1, REACH + 1):
        out += half_weights[step] * ((dz == 0) & (dy == step))
        out += half_weights[step] * ((dy == 0) & (dz == step))
    out += 3.0 * half_weights[0] * ((dy == 0) & (dz == 0))
    return out.astype(np.float32)


def split_constant(x):
    high = x.astype(jnp.bfloat16)
    low = (x - high.astype(np.float32)).astype(jnp.bfloat16)
    return jnp.asarray(high), jnp.asarray(low)


def gram_kernel(b_ref, l_ref, out_ref, acc_ref):
    step = pl.program_id(0)
    rows, planes, lanes = b_ref.shape
    count = l_ref.shape[0]
    b = b_ref[...].reshape(rows * planes, lanes)
    r = jnp.concatenate([b, l_ref[...].reshape(count * planes, lanes)], axis=0)
    bh, bl = split(b)
    rh, rl = split(r)
    nt = ((1,), (1,))
    part = dot(bh, rh, nt) + (dot(bh, rl, nt) + dot(bl, rh, nt))

    @pl.when(step == 0)
    def _():
        acc_ref[...] = part

    @pl.when(step > 0)
    def _():
        acc_ref[...] += part

    @pl.when(step == pl.num_programs(0) - 1)
    def _():
        full = acc_ref[...]
        m, n = full.shape
        same = lax.broadcasted_iota(jnp.int32, (m, n), 0) % planes == lax.broadcasted_iota(jnp.int32, (m, n), 1) % planes
        full = jnp.where(same, full, 0.0)
        left = (
            lax.broadcasted_iota(jnp.int32, (rows, m), 0) == lax.broadcasted_iota(jnp.int32, (rows, m), 1) // planes
        ).astype(jnp.float32)
        right = (
            lax.broadcasted_iota(jnp.int32, (n, n // planes), 0) // planes
            == lax.broadcasted_iota(jnp.int32, (n, n // planes), 1)
        ).astype(jnp.float32)
        half = jnp.dot(left, full, precision=lax.Precision.HIGHEST, preferred_element_type=jnp.float32)
        out_ref[...] = jnp.dot(half, right, precision=lax.Precision.HIGHEST, preferred_element_type=jnp.float32)


def gram(b, later):
    rows, planes, length = b.shape
    count = later.shape[0]
    lanes = 2 * GROUP
    return pl.pallas_call(
        gram_kernel,
        grid=(length // lanes,),
        in_specs=[
            pl.BlockSpec((rows, planes, lanes), lambda i: (0, 0, i)),
            pl.BlockSpec((count, planes, lanes), lambda i: (0, 0, i)),
        ],
        out_specs=pl.BlockSpec((rows, rows + count), lambda i: (0, 0)),
        out_shape=jax.ShapeDtypeStruct((rows, rows + count), jnp.float32),
        scratch_shapes=[pltpu.VMEM((rows * planes, (rows + count) * planes), jnp.float32)],
        compiler_params=pltpu.CompilerParams(vmem_limit_bytes=32 << 20),
        cost_estimate=pl.CostEstimate(
            flops=6 * 256 * 512 * length, bytes_accessed=4 * (rows + count) * planes * length, transcendentals=0
        ),
        name="gram",
    )(b, later)


def stencil_kernel(halos, *refs):
    x_ref = refs[0]
    halo_refs = refs[1 : 1 + halos]
    mats_h, mats_l, wh_ref, wl_ref, v_ref, out_ref = refs[1 + halos :]
    count, planes, length = x_ref.shape
    rows = count * planes
    x = x_ref[...].reshape(rows, length)
    xh, xl = split(x)
    groups = length // GROUP
    parts = [(xh, xl)] + [split(h[...].reshape(rows, length)) for h in halo_refs]
    for g in range(groups):
        lo, hi = max(0, g - 1) * GROUP, min(groups, g + 2) * GROUP
        wlo = lo - (g - 1) * GROUP
        whi = wlo + hi - lo
        wh, wl = wh_ref[wlo:whi, :], wl_ref[wlo:whi, :]
        here = slice(g * GROUP, (g + 1) * GROUP)
        total = dot(xh[:, lo:hi], wh) + (dot(xh[:, lo:hi], wl) + dot(xl[:, lo:hi], wh))
        for j, (ph, pl_) in enumerate(parts):
            total += dot(mats_h[j], ph[:, here]) + (dot(mats_h[j], pl_[:, here]) + dot(mats_l[j], ph[:, here]))
        total = total.reshape(rows // 8, 8, GROUP) + v_ref[:, here] * x[:, here].reshape(rows // 8, 8, GROUP)
        out_ref[:, :, here] = total.reshape(count, planes, GROUP)


def stencil(x, halos, mats, potential, block):
    count, planes, length = x.shape
    size = block * planes
    wide = jnp.stack([jnp.kron(jnp.eye(block, dtype=jnp.float32), m) for m in mats])
    mats_h, mats_l = split_matrix(wide)
    wh, wl = split_constant(yz_matrix())
    v = jnp.concatenate([potential, potential], axis=0)
    n = 1 + len(halos)
    spec = pl.BlockSpec((block, planes, length), lambda i: (i, 0, 0))
    whole2 = lambda i: (0, 0)
    return pl.pallas_call(
        lambda *refs: stencil_kernel(len(halos), *refs),
        grid=(count // block,),
        in_specs=[spec] * n
        + [pl.BlockSpec((n, size, size), lambda i: (0, 0, 0))] * 2
        + [pl.BlockSpec(wh.shape, whole2)] * 2
        + [pl.BlockSpec(v.shape, whole2)],
        out_specs=spec,
        out_shape=jax.ShapeDtypeStruct(x.shape, jnp.float32),
        compiler_params=pltpu.CompilerParams(vmem_limit_bytes=56 << 20),
        cost_estimate=pl.CostEstimate(
            flops=6 * count * planes * length * 1280, bytes_accessed=4 * (n + 1) * x.size, transcendentals=0
        ),
        name="stencil",
    )(x, *halos, mats_h, mats_l, wh, wl, v)


def final_kernel(base_ref, hb_ref, slow_ref, m1h, m1l, m2h, m2l, later_ref, block_ref):
    count, planes, lanes = base_ref.shape
    rows = hb_ref.shape[0] * planes
    hh, hl = split(hb_ref[...].reshape(rows, lanes))
    sh, sl = split(slow_ref[...].reshape(rows, lanes))
    total = dot(m1h[...], hh) + dot(m2h[...], sh)
    total += dot(m1h[...], hl) + dot(m2h[...], sl)
    total += dot(m1l[...], hh) + dot(m2l[...], sh)
    later_ref[...] = base_ref[...] + total[: count * planes].reshape(count, planes, lanes)
    block_ref[...] = total[count * planes :].reshape(block_ref.shape)


def final(base, hb, slow, m1, m2):
    count, planes, length = base.shape
    rows = hb.shape[0]
    own = m1.shape[0] // planes - count
    lanes = 2 * GROUP
    m1h, m1l = split_matrix(m1)
    m2h, m2l = split_matrix(m2)
    along = lambda n: pl.BlockSpec((n, planes, lanes), lambda i: (0, 0, i))
    mat = pl.BlockSpec(m1.shape, lambda i: (0, 0))
    return pl.pallas_call(
        final_kernel,
        grid=(length // lanes,),
        in_specs=[along(count), along(rows), along(rows), mat, mat, mat, mat],
        out_specs=[along(count), along(own)],
        out_shape=[
            jax.ShapeDtypeStruct((count, planes, length), jnp.float32),
            jax.ShapeDtypeStruct((own, planes, length), jnp.float32),
        ],
        compiler_params=pltpu.CompilerParams(vmem_limit_bytes=40 << 20),
        cost_estimate=pl.CostEstimate(
            flops=12 * 320 * 256 * length, bytes_accessed=4 * (2 * count + 2 * rows + own) * planes * length, transcendentals=0
        ),
        name="final",
    )(base, hb, slow, m1h, m1l, m2h, m2l)


def local(blocks, later, potential):
    pair, own_rows, planes, length = blocks.shape
    count = later.shape[0]
    ns, nb = lax.axis_size("space"), lax.axis_size("band")
    s, band = lax.axis_index("space"), lax.axis_index("band")
    cells = planes * ns * length
    own = pair * own_rows
    block_rows = own_rows * nb
    rows = pair * block_rows
    fast_pairs = [(i, i ^ 1) for i in range(ns)]
    slow_pairs = [(i, i + 1) for i in range(1, ns - 1, 2)] + [(i + 1, i) for i in range(1, ns - 1, 2)]

    mine = blocks.reshape(own, planes, length)
    gathered = lax.all_gather(mine, "band").reshape(rows, planes, length)
    slow_mine = lax.ppermute(mine, "space", slow_pairs)
    slow_later = lax.ppermute(later, "space", slow_pairs)
    fast_later = lax.ppermute(later, "space", fast_pairs)
    slow_all = lax.all_gather(slow_mine, "band").reshape(rows, planes, length)
    fast_all = lax.ppermute(gathered, "space", fast_pairs)

    even = s % 2 == 0
    before, within, after = plane_matrix(-planes), plane_matrix(0), plane_matrix(planes)
    fast_mat = jnp.where(even, after, before)
    slow_mat = jnp.where(even, before, after)
    within = jnp.asarray(within)

    products = lax.psum(gram(gathered, later), "space") / cells
    to_block = lambda m: m.reshape(nb, pair, own_rows, -1).swapaxes(0, 1).reshape(rows, -1)
    to_band = lambda m: m.reshape(pair, nb, own_rows, -1).swapaxes(0, 1).reshape(rows, -1)
    products = to_block(products)
    corr = to_block(products[:, :rows].T)
    lower = jnp.linalg.cholesky(corr)
    inverse = lax.linalg.triangular_solve(lower, jnp.eye(rows, dtype=jnp.float32), left_side=True, lower=True)
    hi = lax.Precision.HIGHEST
    weights = jnp.dot(inverse, products[:, rows:], precision=hi)
    coefs = jnp.dot(inverse.T, weights, precision=hi)
    turn = lax.dynamic_slice_in_dim(inverse.reshape(pair, block_rows, rows), band * own_rows, own_rows, 1)
    mix = jnp.concatenate([-coefs.T, turn.reshape(own, rows)], axis=0)
    mix = to_band(mix.T).T
    m1 = jnp.kron(mix, jnp.eye(planes, dtype=jnp.float32))
    m2 = jnp.kron(mix, slow_mat)

    base = stencil(later, [fast_later, slow_later], [within, fast_mat, slow_mat], potential, min(32, count))
    part = stencil(gathered, [fast_all], [within, fast_mat], potential, 32)
    h_later, h_block = final(base, part, slow_all, m1, m2)
    return h_block.reshape(blocks.shape), h_later


def solution(mesh):
    return jax.shard_map(
        local,
        mesh=mesh,
        in_specs=(P(None, "band", "space", None), P("band", "space", None), P("space", None)),
        out_specs=(P(None, "band", "space", None), P("band", "space", None)),
        check_vma=False,
    )
```

```python
import functools

import jax
import jax.numpy as jnp
import numpy as np
from jax import lax
from jax.experimental import pallas as pl
from jax.experimental.pallas import tpu as pltpu
from jax.sharding import PartitionSpec as P

NZ = 96
REACH = 4
LANE = 128

stencil_weights = (-205.0 / 72.0, 8.0 / 5.0, -1.0 / 5.0, 8.0 / 315.0, -1.0 / 560.0)
half_weights = tuple(-0.5 * w for w in stencil_weights)

GROUP = 4 * NZ
HIGHEST = lax.Precision.HIGHEST


def split(x):
    high = x.astype(jnp.bfloat16)
    low = (x - high.astype(jnp.float32)).astype(jnp.bfloat16)
    return high, low


def dot(a, b, dims=((1,), (0,))):
    return lax.dot_general(a, b, (dims, ((), ())), preferred_element_type=jnp.float32)


def exact(a, b, dims=((1,), (0,))):
    return lax.dot_general(a, b, (dims, ((), ())), precision=HIGHEST, preferred_element_type=jnp.float32)


def plane_matrix(offset):
    out = np.zeros((REACH, REACH), np.float32)
    for p in range(REACH):
        for q in range(REACH):
            shift = abs(q + offset - p)
            if 1 <= shift <= REACH:
                out[p, q] = half_weights[shift]
    return out


def spread_variants(left_of_variant, count):
    eye = np.eye(count, dtype=np.float32)
    return np.stack([np.concatenate([np.kron(eye, m) for m in ms], axis=1) for ms in left_of_variant])


def z_matrix():
    a = np.arange(GROUP)[:, None]
    o = np.arange(GROUP)[None, :]
    dz = np.abs(a - o)
    same = a // NZ == o // NZ
    out = np.zeros((GROUP, GROUP), np.float64)
    for step in range(1, REACH + 1):
        out += half_weights[step] * (same & (dz == step))
    out += 3.0 * half_weights[0] * (dz == 0)
    return out.astype(np.float32)


def split_constant(x):
    high = x.astype(jnp.bfloat16)
    low = (x - high.astype(np.float32)).astype(jnp.bfloat16)
    return jnp.asarray(high), jnp.asarray(low)


def rows_of(ref):
    count, planes, lanes = ref.shape
    return ref[...].reshape(count * planes, lanes)


def one_hot(shape, row, column):
    r = lax.broadcasted_iota(jnp.int32, shape, 0)
    c = lax.broadcasted_iota(jnp.int32, shape, 1)
    return (row(r) == column(c)).astype(jnp.float32)


def gram_kernel(slots, *refs):
    b_refs, l_ref, out_ref, acc_ref = refs[:slots], refs[slots], refs[slots + 1], refs[slots + 2]
    step = pl.program_id(0)
    planes = l_ref.shape[1]
    bh, bl = split(jnp.concatenate([rows_of(r) for r in b_refs], axis=0))
    lh, ll = split(rows_of(l_ref))
    rh = jnp.concatenate([bh, lh], axis=0)
    rl = jnp.concatenate([bl, ll], axis=0)
    nt = ((1,), (1,))
    part = dot(bh, rh, nt) + (dot(bh, rl, nt) + dot(bl, rh, nt))

    @pl.when(step == 0)
    def _():
        acc_ref[...] = part

    @pl.when(step > 0)
    def _():
        acc_ref[...] += part

    @pl.when(step == pl.num_programs(0) - 1)
    def _():
        full = acc_ref[...]
        m, n = full.shape
        full = full * one_hot((m, n), lambda r: r % planes, lambda c: c % planes)
        left = one_hot((m // planes, m), lambda r: r, lambda c: c // planes)
        right = one_hot((n, n // planes), lambda r: r // planes, lambda c: c)
        out_ref[...] = exact(exact(left, full), right)


def gram(slots, later):
    own, planes, length = slots[0].shape
    rows = own * len(slots)
    count = later.shape[0]
    lanes = 2 * GROUP
    along = lambda n: pl.BlockSpec((n, planes, lanes), lambda i: (0, 0, i))
    return pl.pallas_call(
        functools.partial(gram_kernel, len(slots)),
        grid=(length // lanes,),
        in_specs=[along(own)] * len(slots) + [along(count)],
        out_specs=pl.BlockSpec((rows, rows + count), lambda i: (0, 0)),
        out_shape=jax.ShapeDtypeStruct((rows, rows + count), jnp.float32),
        scratch_shapes=[pltpu.VMEM((rows * planes, (rows + count) * planes), jnp.float32)],
        compiler_params=pltpu.CompilerParams(vmem_limit_bytes=32 << 20),
        cost_estimate=pl.CostEstimate(
            flops=8_000_000_000, bytes_accessed=4 * (rows + count) * planes * length, transcendentals=0
        ),
        name="gram",
    )(*slots, later)


def mix_kernel(band_ref, slow_ref, prod_ref, m1h, m1l, m2h, m2l, work_ref, *, cells, bands, own_rows, count):
    rows = prod_ref.shape[0]
    block_rows = bands * own_rows
    own = 2 * own_rows
    planes = REACH
    band = band_ref[0]

    def home(r):
        slot, inside = r // own, r % own
        held = (slot + band) % bands
        return (inside // own_rows) * block_rows + held * own_rows + inside % own_rows

    place = one_hot((rows, rows), lambda r: r, home)
    products = exact(place, prod_ref[...] * (1.0 / cells))
    corr = exact(products[:, :rows], place, ((1,), (1,)))
    eye = one_hot((rows, rows), lambda r: r, lambda c: c)
    work_ref[...] = jnp.concatenate([corr, eye, products[:, rows:]], axis=1)
    width = work_ref.shape[1]
    row_id = lax.broadcasted_iota(jnp.int32, (rows, 1), 0)
    col_id = lax.broadcasted_iota(jnp.int32, (rows, width), 1)

    def eliminate(j, _):
        table = work_ref[...]
        pivot_row = work_ref[pl.ds(j, 1), :]
        column = jnp.sum(jnp.where(col_id == j, table, 0.0), axis=1, keepdims=True)
        pivot = jnp.sum(jnp.where(row_id == j, column, 0.0), axis=0, keepdims=True)
        scale = lax.rsqrt(pivot)
        scale = scale * (1.5 - 0.5 * pivot * scale * scale)
        scaled = pivot_row * scale
        factor = jnp.where(row_id > j, column * scale, 0.0)
        work_ref[...] = jnp.where(row_id == j, scaled, table - factor * scaled)
        return 0

    lax.fori_loop(0, rows, eliminate, 0)
    table = work_ref[...]
    inverse = table[:, rows : 2 * rows]
    weights = table[:, 2 * rows :]
    tn = ((0,), (0,))
    coefs = exact(weights, inverse, tn)
    mine = one_hot((own, rows), lambda r: (r // own_rows) * block_rows + band * own_rows + r % own_rows, lambda c: c)
    mix = jnp.concatenate([-coefs, exact(mine, inverse)], axis=0)
    mix = exact(mix, place)
    outs = count + own
    tall = one_hot((outs * planes, outs), lambda r: r // planes, lambda c: c)
    wide = one_hot((rows, rows * planes), lambda r: r, lambda c: c // planes)
    spread = exact(exact(tall, mix), wide)
    p = lax.broadcasted_iota(jnp.int32, spread.shape, 0) % planes
    q = lax.broadcasted_iota(jnp.int32, spread.shape, 1) % planes
    first = jnp.where(p == q, spread, 0.0)
    pattern = jnp.zeros_like(spread)
    for a in range(planes):
        for b in range(planes):
            pattern = jnp.where((p == a) & (q == b), slow_ref[a, b], pattern)
    second = spread * pattern
    m1h[...], m1l[...] = split(first)
    m2h[...], m2l[...] = split(second)


def mix(products, band, slow_mat, cells, bands, own_rows, count):
    rows = products.shape[0]
    planes = REACH
    out = jax.ShapeDtypeStruct(((count + 2 * own_rows) * planes, rows * planes), jnp.bfloat16)
    return pl.pallas_call(
        functools.partial(mix_kernel, cells=cells, bands=bands, own_rows=own_rows, count=count),
        in_specs=[
            pl.BlockSpec(memory_space=pltpu.SMEM),
            pl.BlockSpec(memory_space=pltpu.SMEM),
            pl.BlockSpec(memory_space=pltpu.VMEM),
        ],
        out_specs=[pl.BlockSpec(memory_space=pltpu.VMEM)] * 4,
        out_shape=[out] * 4,
        scratch_shapes=[pltpu.VMEM((rows, 2 * rows + count), jnp.float32)],
        compiler_params=pltpu.CompilerParams(vmem_limit_bytes=32 << 20),
        cost_estimate=pl.CostEstimate(flops=10_000_000_000, bytes_accessed=1 << 20, transcendentals=0),
        name="mix",
    )(band.reshape(1), slow_mat, products)


def along_y(x):
    n = len(x)
    lane = lax.broadcasted_iota(jnp.int32, (8, LANE), 1)
    zero = jnp.zeros((8, LANE), jnp.float32)
    r32 = [pltpu.roll(v, 32, 1) for v in x]
    r64 = [pltpu.roll(v, 64, 1) for v in x]
    r96 = [pltpu.roll(v, 96, 1) for v in x]
    at = lambda list_, i: list_[i] if 0 <= i < n else zero
    below32, below64, below96 = lane < 32, lane < 64, lane < 96
    out = []
    for i in range(n):
        one = jnp.where(below32, at(r32, i), at(r32, i + 1)) + jnp.where(below96, at(r96, i - 1), at(r96, i))
        two = jnp.where(below64, at(r64, i + 1), at(r64, i + 2)) + jnp.where(below64, at(r64, i - 2), at(r64, i - 1))
        three = jnp.where(below96, at(r96, i + 2), at(r96, i + 3)) + jnp.where(below32, at(r32, i - 3), at(r32, i - 2))
        four = at(x, i + 3) + at(x, i - 3)
        out.append(half_weights[1] * one + half_weights[2] * two + half_weights[3] * three + half_weights[4] * four)
    return out


def stencil_kernel(x_ref, halo_ref, mh_ref, ml_ref, zh_ref, zl_ref, v_ref, out_ref, flat_ref, acc_ref):
    count, planes, length = x_ref.shape
    rows = count * planes
    groups = length // GROUP
    flat_ref[...] = rows_of(x_ref)
    vectors = length // LANE

    def eight(t, _):
        at = pl.ds(pl.multiple_of(t * 8, 8), 8)
        x = [flat_ref[at, i * LANE : (i + 1) * LANE] for i in range(vectors)]
        ys = along_y(x)
        for i in range(vectors):
            acc_ref[at, i * LANE : (i + 1) * LANE] = ys[i] + v_ref[:, i * LANE : (i + 1) * LANE] * x[i]
        return 0

    lax.fori_loop(0, rows // 8, eight, 0)
    zh, zl = zh_ref[...], zl_ref[...]
    mh, ml = mh_ref[...], ml_ref[...]
    for g in range(groups):
        here = slice(g * GROUP, (g + 1) * GROUP)
        xh, xl = split(flat_ref[:, here])
        hh, hl = split(halo_ref[:, :, here].reshape(rows, GROUP))
        both_h = jnp.concatenate([xh, hh], axis=0)
        both_l = jnp.concatenate([xl, hl], axis=0)
        total = dot(xh, zh) + dot(mh, both_h)
        total += dot(xh, zl) + dot(mh, both_l)
        total += dot(xl, zh) + dot(ml, both_h)
        total += acc_ref[:, here]
        out_ref[:, :, here] = total.reshape(count, planes, GROUP)


def stencil(x, halo, odd, potential, block):
    count, planes, length = x.shape
    size = block * planes
    within = plane_matrix(0)
    mh, ml = split_constant(spread_variants([(within, plane_matrix(planes)), (within, plane_matrix(-planes))], block))
    zh, zl = split_constant(z_matrix())
    v = jnp.concatenate([potential, potential], axis=0)
    spec = pl.BlockSpec((block, planes, length), lambda i, odd: (i, 0, 0))
    picked = pl.BlockSpec((pl.squeezed,) + mh.shape[1:], lambda i, odd: (odd[0], 0, 0))
    fixed = lambda a: pl.BlockSpec(a.shape, lambda i, odd: (0, 0))
    return pl.pallas_call(
        lambda odd_ref, *refs: stencil_kernel(*refs),
        grid_spec=pltpu.PrefetchScalarGridSpec(
            num_scalar_prefetch=1,
            grid=(count // block,),
            in_specs=[spec, spec, picked, picked] + [fixed(a) for a in (zh, zl, v)],
            out_specs=spec,
            scratch_shapes=[pltpu.VMEM((size, length), jnp.float32)] * 2,
        ),
        out_shape=jax.ShapeDtypeStruct(x.shape, jnp.float32),
        compiler_params=pltpu.CompilerParams(vmem_limit_bytes=48 << 20),
        cost_estimate=pl.CostEstimate(flops=100_000_000 * count, bytes_accessed=12 * x.size, transcendentals=0),
        name="stencil",
    )(odd, x, halo, mh, ml, zh, zl, v)


def add_slow_kernel(kind_ref, two_ref, base_ref, one_hop_ref, two_hop_ref, mh_ref, ml_ref, out_ref):
    count, planes, lanes = base_ref.shape
    rows = count * planes
    halo = jnp.where(two_ref[0] > 0, two_hop_ref[...], one_hop_ref[...]).reshape(rows, lanes)
    hh, hl = split(halo)
    mh, ml = mh_ref[...], ml_ref[...]
    total = dot(mh, hh) + (dot(mh, hl) + dot(ml, hh))
    out_ref[...] = base_ref[...] + total.reshape(count, planes, lanes)


def add_slow(kind, two, base, one_hop, two_hop):
    count, planes, length = base.shape
    none = np.zeros((planes, planes), np.float32)
    mh, ml = split_constant(spread_variants([(plane_matrix(-planes),), (plane_matrix(planes),), (none,)], count))
    lanes = 2 * GROUP
    along = pl.BlockSpec((count, planes, lanes), lambda i, kind, two: (0, 0, i))
    picked = pl.BlockSpec((pl.squeezed,) + mh.shape[1:], lambda i, kind, two: (kind[0], 0, 0))
    return pl.pallas_call(
        add_slow_kernel,
        grid_spec=pltpu.PrefetchScalarGridSpec(
            num_scalar_prefetch=2,
            grid=(length // lanes,),
            in_specs=[along, along, along, picked, picked],
            out_specs=along,
        ),
        out_shape=jax.ShapeDtypeStruct(base.shape, jnp.float32),
        compiler_params=pltpu.CompilerParams(vmem_limit_bytes=32 << 20),
        cost_estimate=pl.CostEstimate(flops=3_000_000_000, bytes_accessed=16 * base.size, transcendentals=0),
        name="add_slow",
    )(kind, two, base, one_hop, two_hop, mh, ml)


def final_kernel(slots, base_ref, *refs):
    hb_refs, slow_refs = refs[:slots], refs[slots : 2 * slots]
    m1h, m1l, m2h, m2l, later_ref, block_ref = refs[2 * slots :]
    count, planes, lanes = base_ref.shape
    hh, hl = split(jnp.concatenate([rows_of(r) for r in hb_refs], axis=0))
    sh, sl = split(jnp.concatenate([rows_of(r) for r in slow_refs], axis=0))
    total = dot(m1h[...], hh) + dot(m2h[...], sh)
    total += dot(m1h[...], hl) + dot(m2h[...], sl)
    total += dot(m1l[...], hh) + dot(m2l[...], sh)
    later_ref[...] = base_ref[...] + total[: count * planes].reshape(count, planes, lanes)
    block_ref[...] = total[count * planes :].reshape(block_ref.shape)


def final(base, hb, slow, mats):
    count, planes, length = base.shape
    own = hb[0].shape[0]
    lanes = 2 * GROUP
    along = lambda n: pl.BlockSpec((n, planes, lanes), lambda i: (0, 0, i))
    fixed = pl.BlockSpec(mats[0].shape, lambda i: (0, 0))
    return pl.pallas_call(
        functools.partial(final_kernel, len(hb)),
        grid=(length // lanes,),
        in_specs=[along(count)] + [along(own)] * (2 * len(hb)) + [fixed] * 4,
        out_specs=[along(count), along(own)],
        out_shape=[
            jax.ShapeDtypeStruct((count, planes, length), jnp.float32),
            jax.ShapeDtypeStruct((own, planes, length), jnp.float32),
        ],
        compiler_params=pltpu.CompilerParams(vmem_limit_bytes=40 << 20),
        cost_estimate=pl.CostEstimate(flops=6_000_000_000, bytes_accessed=20 * base.size, transcendentals=0),
        name="final",
    )(base, *hb, *slow, *mats)


def after(x, *others):
    return lax.optimization_barrier((x,) + others)[0]


def local(blocks, later, potential):
    pair, own_rows, planes, length = blocks.shape
    count = later.shape[0]
    ns, nb = lax.axis_size("space"), lax.axis_size("band")
    s, band = lax.axis_index("space"), lax.axis_index("band")
    cells = planes * ns * length
    own = pair * own_rows
    both = ("space", "band")

    fast_pairs = [(i, i ^ 1) for i in range(ns)]
    near = [(i, i + 1) for i in range(1, ns - 1, 4)]
    near += [(j, i) for i, j in near]
    across = range(3, ns - 1, 4)
    far = [(i, i + 1) for i in across] + [(i + 1, i) for i in across]
    hop_one = [(i, i + 4) for i in across] + [(i + 1, i - 3) for i in across]
    hop_two = [(i + 4, i + 1) for i in across] + [(i - 3, i) for i in across]
    is_far = ((s % 4 == 3) & (s < ns - 1)) | ((s % 4 == 0) & (s > 0))
    ring = [(b + 1, b) for b in range(nb - 1)] + [(0, nb - 1)]
    far_pairs = [(i * nb + b, j * nb + b) for i, j in far for b in range(nb)]

    odd = (s % 2).astype(jnp.int32).reshape(1)
    edge = (s == 0) | (s == ns - 1)
    kind = jnp.where(edge, 2, odd)
    before, behind = plane_matrix(-planes), plane_matrix(planes)
    slow_mat = jnp.where(edge, 0.0, jnp.where(s % 2 == 0, before, behind))

    mine = blocks.reshape(own, planes, length)
    slots, slow = [None] * nb, [None] * nb
    slots[0] = mine
    up = lambda x: lax.ppermute(x, "band", ring)
    down = lambda x: lax.ppermute(x, "band", [(j, i) for i, j in ring])
    swap = lambda x: lax.ppermute(x, "space", fast_pairs)
    step_up = lambda x: lax.ppermute(x, both, far_pairs + [(i * nb + b, i * nb + c) for i, _ in near for b, c in ring])
    step_down = lambda x: lax.ppermute(x, both, far_pairs + [(i * nb + c, i * nb + b) for i, _ in near for b, c in ring])

    slots[1], slots[-1] = up(mine), down(mine)
    fast_later, fast_mine = swap(later), swap(mine)
    slow[0] = lax.ppermute(mine, "space", near + far)
    one_hop = lax.ppermute(later, "space", near + hop_one)
    base = stencil(later, fast_later, odd, potential, min(32, count))
    hb = [None] * nb
    hb[0] = stencil(mine, fast_mine, odd, potential, own)
    token = (base, hb[0])
    fast = [fast_mine] + [None] * (nb - 1)
    order = []
    lo, hi = 1, nb - 1
    while lo <= hi:
        order += [lo] if lo == hi else [lo, hi]
        lo, hi = lo + 1, hi - 1
    for k in order:
        if slots[k] is None:
            low = k <= nb // 2
            slots[k] = (up if low else down)(after(slots[k - 1] if low else slots[k + 1], *token))
    for k in order:
        fast[k] = swap(slots[k])
    two_hop = lax.ppermute(one_hop, "space", hop_two)
    gathered = slots[nb // 2]
    for k in order:
        low = k <= nb // 2
        kept = jnp.where(is_far, slots[k], slow[k - 1] if low else slow[(k + 1) % nb])
        slow[k] = (step_up if low else step_down)(after(kept, gathered))
    for k in order:
        hb[k] = stencil(slots[k], fast[k], odd, potential, own)

    products = gram(slots, later)
    reach = 1
    while reach < ns:
        products = products + lax.ppermute(products, "space", [(i, i ^ reach) for i in range(ns)])
        reach *= 2
    mats = mix(products, band, slow_mat, cells, nb, own_rows, count)
    base = add_slow(kind, is_far.astype(jnp.int32).reshape(1), base, one_hop, two_hop)
    h_later, h_block = final(base, hb, slow, mats)
    return h_block.reshape(blocks.shape), h_later


def solution(mesh):
    return jax.shard_map(
        local,
        mesh=mesh,
        in_specs=(P(None, "band", "space", None), P("band", "space", None), P("space", None)),
        out_specs=(P(None, "band", "space", None), P("band", "space", None)),
        check_vma=False,
    )
```

```python
import functools

import jax
import jax.numpy as jnp
import numpy as np
from jax import lax
from jax.experimental import pallas as pl
from jax.experimental.pallas import tpu as pltpu
from jax.sharding import PartitionSpec as P

NZ = 96
REACH = 4
LANE = 128
VMEM = 60 << 20

stencil_weights = (-205.0 / 72.0, 8.0 / 5.0, -1.0 / 5.0, 8.0 / 315.0, -1.0 / 560.0)
half_weights = tuple(-0.5 * w for w in stencil_weights)

GROUP = 4 * NZ
HIGHEST = lax.Precision.HIGHEST


def split(x):
    high = x.astype(jnp.bfloat16)
    low = (x - high.astype(jnp.float32)).astype(jnp.bfloat16)
    return high, low


def thrice(m):
    high, low = split(m)
    return jnp.concatenate([high, high, low], axis=1)


def stacked(x):
    high, low = split(x)
    return jnp.concatenate([high, low, high], axis=0)


def dot(a, b, dims=((1,), (0,))):
    return lax.dot_general(a, b, (dims, ((), ())), preferred_element_type=jnp.float32)


def exact(a, b, dims=((1,), (0,))):
    return lax.dot_general(a, b, (dims, ((), ())), precision=HIGHEST, preferred_element_type=jnp.float32)


def plane_matrix(offset):
    out = np.zeros((REACH, REACH), np.float32)
    for p in range(REACH):
        for q in range(REACH):
            shift = abs(q + offset - p)
            if 1 <= shift <= REACH:
                out[p, q] = half_weights[shift]
    return out


def spread_variants(left_of_variant, count):
    eye = np.eye(count, dtype=np.float32)
    return np.stack([np.concatenate([np.kron(eye, m) for m in ms], axis=1) for ms in left_of_variant])


def z_matrix():
    a = np.arange(GROUP)[:, None]
    o = np.arange(GROUP)[None, :]
    dz = np.abs(a - o)
    same = a // NZ == o // NZ
    out = np.zeros((GROUP, GROUP), np.float64)
    for step in range(1, REACH + 1):
        out += half_weights[step] * (same & (dz == step))
    out += 3.0 * half_weights[0] * (dz == 0)
    return out.astype(np.float32)


def thrice_constant(x):
    high = x.astype(jnp.bfloat16)
    low = (x - high.astype(np.float32)).astype(jnp.bfloat16)
    return jnp.asarray(np.concatenate([high, high, low], axis=-1))


def split_constant(x):
    high = x.astype(jnp.bfloat16)
    low = (x - high.astype(np.float32)).astype(jnp.bfloat16)
    return jnp.asarray(high), jnp.asarray(low)


def rows_of(ref):
    count, planes, lanes = ref.shape
    return ref[...].reshape(count * planes, lanes)


def one_hot(shape, row, column):
    r = lax.broadcasted_iota(jnp.int32, shape, 0)
    c = lax.broadcasted_iota(jnp.int32, shape, 1)
    return (row(r) == column(c)).astype(jnp.float32)


def gram_kernel(slots, *refs):
    b_refs, l_ref, out_ref, acc_ref = refs[:slots], refs[slots], refs[slots + 1], refs[slots + 2]
    step = pl.program_id(0)
    own, planes = b_refs[0].shape[:2]
    bh, bl = split(jnp.concatenate([rows_of(r) for r in b_refs], axis=0))
    lh, ll = split(rows_of(l_ref))
    rh = jnp.concatenate([bh, lh], axis=0)
    rl = jnp.concatenate([bl, ll], axis=0)
    part = dot(jnp.concatenate([bh, bh, bl], axis=1), jnp.concatenate([rh, rl, rh], axis=1), ((1,), (1,)))

    @pl.when(step == 0)
    def _():
        acc_ref[...] = part

    @pl.when(step > 0)
    def _():
        acc_ref[...] += part

    @pl.when(step == pl.num_programs(0) - 1)
    def _():
        full = acc_ref[...]
        m, n = full.shape
        full = full * one_hot((m, n), lambda r: r % planes, lambda c: c % planes)
        left = one_hot((m // planes, m), lambda r: r, lambda c: c // planes)
        place = lambda r: r // planes + jnp.where(r // planes < own * slots, 0, own)
        right = one_hot((n, out_ref.shape[1]), place, lambda c: c)
        out_ref[...] = exact(exact(left, full), right)


def gram(slots, later):
    own, planes, length = slots[0].shape
    rows = own * len(slots)
    count = later.shape[0]
    lanes = 2 * GROUP
    along = lambda n: pl.BlockSpec((n, planes, lanes), lambda i: (0, 0, i))
    return pl.pallas_call(
        functools.partial(gram_kernel, len(slots)),
        grid=(length // lanes,),
        in_specs=[along(own)] * len(slots) + [along(count)],
        out_specs=pl.BlockSpec((rows, rows + own + count), lambda i: (0, 0)),
        out_shape=jax.ShapeDtypeStruct((rows, rows + own + count), jnp.float32),
        scratch_shapes=[pltpu.VMEM((rows * planes, (rows + count) * planes), jnp.float32)],
        compiler_params=pltpu.CompilerParams(vmem_limit_bytes=VMEM),
        cost_estimate=pl.CostEstimate(
            flops=8_000_000_000, bytes_accessed=4 * (rows + count) * planes * length, transcendentals=0
        ),
        name="gram",
    )(*slots, later)


def gram_last_kernel(slots, *refs):
    b_refs, l_ref, known_ref, out_ref, acc_ref = refs[:slots], refs[slots], *refs[slots + 1 :]
    step = pl.program_id(0)
    own, planes = b_refs[0].shape[:2]
    size = own * planes
    rh, rl = split(jnp.concatenate([rows_of(r) for r in b_refs] + [rows_of(l_ref)], axis=0))
    here = slice(size * (slots - 1), size * slots)
    weights = jnp.concatenate([rh[here], rl[here]], axis=0)
    part = dot(jnp.concatenate([rh, rl], axis=0), weights, ((1,), (1,)))

    @pl.when(step == 0)
    def _():
        acc_ref[...] = part

    @pl.when(step > 0)
    def _():
        acc_ref[...] += part

    @pl.when(step == pl.num_programs(0) - 1)
    def _():
        n = rh.shape[0]
        full = acc_ref[...]
        full = full[:n] + full[n:]
        full = full * one_hot(full.shape, lambda r: r % planes, lambda c: c % planes)
        left = one_hot((own, full.shape[1]), lambda r: r, lambda c: (c % size) // planes)
        right = one_hot((n, n // planes), lambda r: r // planes, lambda c: c)
        new = exact(exact(left, full, ((1,), (1,))), right)
        rows = own * slots
        for copy in range(out_ref.shape[0] // rows):
            out_ref[copy * rows : (copy + 1) * rows - own, :] = known_ref[...]
            out_ref[(copy + 1) * rows - own : (copy + 1) * rows, :] = new


def gram_last(slots, later, known, copies):
    own, planes, length = slots[0].shape
    rows = own * len(slots)
    count = later.shape[0]
    lanes = 2 * GROUP
    along = lambda n: pl.BlockSpec((n, planes, lanes), lambda i: (0, 0, i))
    return pl.pallas_call(
        functools.partial(gram_last_kernel, len(slots)),
        grid=(length // lanes,),
        in_specs=[along(own)] * len(slots) + [along(count), pl.BlockSpec(known.shape, lambda i: (0, 0))],
        out_specs=pl.BlockSpec((copies * rows, rows + count), lambda i: (0, 0)),
        out_shape=jax.ShapeDtypeStruct((copies * rows, rows + count), jnp.float32),
        scratch_shapes=[pltpu.VMEM((2 * (rows + count) * planes, 2 * own * planes), jnp.float32)],
        compiler_params=pltpu.CompilerParams(vmem_limit_bytes=VMEM),
        cost_estimate=pl.CostEstimate(
            flops=4_000_000_000, bytes_accessed=4 * (rows + count) * planes * length, transcendentals=0
        ),
        name="gram_last",
    )(*slots, later, known)


def mix_kernel(band_ref, slow_ref, prod_ref, out_ref, *, cells, bands, own_rows, count, order):
    own = 2 * own_rows
    rows = bands * own
    block_rows = bands * own_rows
    planes = REACH
    band = band_ref[0]
    products = prod_ref[0, :rows, :]
    for d in range(1, prod_ref.shape[0]):
        products = products + prod_ref[d, :rows, :]
    products = products * (1.0 / cells)

    def home(r):
        turn, inside = r // own, r % own
        slot = jnp.zeros_like(r)
        for t, k in enumerate(order):
            slot = jnp.where(turn == t, k, slot)
        held = (slot + band) % bands
        return (inside // own_rows) * block_rows + held * own_rows + inside % own_rows

    place = one_hot((rows, rows), lambda r: r, home)
    last = rows - own
    flip = exact(products[last:, :last], one_hot((own, own), lambda r: r, lambda c: c), ((0,), (0,)))
    corr = jnp.concatenate(
        [jnp.concatenate([products[:last, :last], flip], axis=1), products[last:, :rows]], axis=0
    )
    corr = exact(exact(place, corr), place, ((1,), (1,)))
    eye = one_hot((rows, rows), lambda r: r, lambda c: c)
    table = jnp.concatenate([corr, eye, exact(place, products[:, rows:])], axis=1)
    tiles = [table[t : t + 8] for t in range(0, rows, 8)]
    row_id = lax.broadcasted_iota(jnp.int32, (8, 1), 0)
    for j in range(rows):
        t = j // 8
        pivot_row = tiles[t][j % 8 : j % 8 + 1]
        step = pivot_row * (1.0 / pivot_row[:, j : j + 1])
        tiles[t] = tiles[t] - jnp.where(row_id > j % 8, tiles[t][:, j : j + 1], 0.0) * step
        for u in range(t + 1, len(tiles)):
            tiles[u] = tiles[u] - tiles[u][:, j : j + 1] * step
    table = jnp.concatenate(tiles, axis=0)
    pivots = jnp.sum(table[:, :rows] * eye, axis=1, keepdims=True)
    scale = lax.rsqrt(pivots)
    scale = scale * (1.5 - 0.5 * pivots * scale * scale)
    inverse = table[:, rows : 2 * rows] * scale
    weights = table[:, 2 * rows :] * scale
    coefs = exact(weights, inverse, ((0,), (0,)))
    mine = one_hot((own, rows), lambda r: (r // own_rows) * block_rows + band * own_rows + r % own_rows, lambda c: c)
    mix = jnp.concatenate([-coefs, exact(mine, inverse)], axis=0)
    mix = exact(mix, place)
    outs = count + own
    tall = one_hot((outs * planes, outs), lambda r: r // planes, lambda c: c)
    wide = one_hot((rows, rows * planes), lambda r: r, lambda c: c // planes)
    spread = exact(exact(tall, mix), wide)
    p = lax.broadcasted_iota(jnp.int32, (8, spread.shape[1]), 0) % planes
    q = lax.broadcasted_iota(jnp.int32, (8, spread.shape[1]), 1) % planes
    pattern = jnp.zeros(p.shape, jnp.float32)
    for a in range(planes):
        for b in range(planes):
            pattern = jnp.where((p == a) & (q == b), slow_ref[a, b], pattern)
    same = (p == q).astype(jnp.float32)
    spread = spread.reshape(outs * planes // 8, 8, rows * planes)
    first = (spread * same[None]).reshape(outs * planes, rows * planes)
    second = (spread * pattern[None]).reshape(outs * planes, rows * planes)
    out_ref[...] = thrice(jnp.concatenate([first, second], axis=1))


def mix(products, band, slow_mat, cells, bands, own_rows, count, order):
    own = 2 * own_rows
    rows = bands * own
    planes = REACH
    return pl.pallas_call(
        functools.partial(mix_kernel, cells=cells, bands=bands, own_rows=own_rows, count=count, order=order),
        in_specs=[
            pl.BlockSpec(memory_space=pltpu.SMEM),
            pl.BlockSpec(memory_space=pltpu.SMEM),
            pl.BlockSpec(memory_space=pltpu.VMEM),
        ],
        out_specs=pl.BlockSpec(memory_space=pltpu.VMEM),
        out_shape=jax.ShapeDtypeStruct(((count + own) * planes, 6 * rows * planes), jnp.bfloat16),
        compiler_params=pltpu.CompilerParams(vmem_limit_bytes=VMEM),
        cost_estimate=pl.CostEstimate(flops=10_000_000_000, bytes_accessed=1 << 20, transcendentals=0),
        name="mix",
    )(band.reshape(1), slow_mat, products)


def along_y(x):
    n = len(x)
    lane = lax.broadcasted_iota(jnp.int32, (8, LANE), 1)
    zero = jnp.zeros((8, LANE), jnp.float32)
    r32 = [pltpu.roll(v, 32, 1) for v in x]
    r64 = [pltpu.roll(v, 64, 1) for v in x]
    r96 = [pltpu.roll(v, 96, 1) for v in x]
    at = lambda list_, i: list_[i] if 0 <= i < n else zero
    below32, below64, below96 = lane < 32, lane < 64, lane < 96
    out = []
    for i in range(n):
        one = jnp.where(below32, at(r32, i), at(r32, i + 1)) + jnp.where(below96, at(r96, i - 1), at(r96, i))
        two = jnp.where(below64, at(r64, i + 1), at(r64, i + 2)) + jnp.where(below64, at(r64, i - 2), at(r64, i - 1))
        three = jnp.where(below96, at(r96, i + 2), at(r96, i + 3)) + jnp.where(below32, at(r32, i - 3), at(r32, i - 2))
        four = at(x, i + 3) + at(x, i - 3)
        out.append(half_weights[1] * one + half_weights[2] * two + half_weights[3] * three + half_weights[4] * four)
    return out


def stencil_kernel(x_ref, halo_ref, m_ref, z_ref, v_ref, out_ref, flat_ref, acc_ref):
    count, planes, length = x_ref.shape
    rows = count * planes
    groups = length // GROUP
    flat_ref[...] = rows_of(x_ref)
    vectors = length // LANE

    def eight(t, _):
        at = pl.ds(pl.multiple_of(t * 8, 8), 8)
        x = [flat_ref[at, i * LANE : (i + 1) * LANE] for i in range(vectors)]
        ys = along_y(x)
        for i in range(vectors):
            acc_ref[at, i * LANE : (i + 1) * LANE] = ys[i] + v_ref[:, i * LANE : (i + 1) * LANE] * x[i]
        return 0

    lax.fori_loop(0, rows // 8, eight, 0)
    for g in range(groups):
        here = slice(g * GROUP, (g + 1) * GROUP)
        x = flat_ref[:, here]
        xh, xl = split(x)
        total = dot(jnp.concatenate([xh, xl, xh], axis=1), z_ref[...])
        total += dot(m_ref[...], stacked(jnp.concatenate([x, halo_ref[:, :, here].reshape(rows, GROUP)], axis=0)))
        total += acc_ref[:, here]
        out_ref[:, :, here] = total.reshape(count, planes, GROUP)


def stencil(x, halo, odd, potential, block):
    count, planes, length = x.shape
    size = block * planes
    within = plane_matrix(0)
    m = thrice_constant(spread_variants([(within, plane_matrix(planes)), (within, plane_matrix(-planes))], block))
    zh, zl = split_constant(z_matrix())
    z = jnp.concatenate([zh, zh, zl], axis=0)
    v = jnp.concatenate([potential, potential], axis=0)
    spec = pl.BlockSpec((block, planes, length), lambda i, odd: (i, 0, 0))
    picked = pl.BlockSpec((pl.squeezed,) + m.shape[1:], lambda i, odd: (odd[0], 0, 0))
    fixed = lambda a: pl.BlockSpec(a.shape, lambda i, odd: (0, 0))
    return pl.pallas_call(
        lambda odd_ref, *refs: stencil_kernel(*refs),
        grid_spec=pltpu.PrefetchScalarGridSpec(
            num_scalar_prefetch=1,
            grid=(count // block,),
            in_specs=[spec, spec, picked, fixed(z), fixed(v)],
            out_specs=spec,
            scratch_shapes=[pltpu.VMEM((size, length), jnp.float32)] * 2,
        ),
        out_shape=jax.ShapeDtypeStruct(x.shape, jnp.float32),
        compiler_params=pltpu.CompilerParams(vmem_limit_bytes=VMEM),
        cost_estimate=pl.CostEstimate(flops=100_000_000 * count, bytes_accessed=12 * x.size, transcendentals=0),
        name="stencil",
    )(odd, x, halo, m, z, v)


def final_kernel(slots, kind_ref, far_ref, base_ref, near_later, far_later, *refs):
    hb_refs, refs = refs[:slots], refs[slots:]
    slow_ref, near_refs, far_refs = refs[0], refs[1:slots], refs[slots : 2 * slots - 1]
    k_ref, m_ref, later_ref, block_ref = refs[2 * slots - 1 :]
    count, planes, lanes = base_ref.shape
    rows = count * planes
    is_far = far_ref[0] > 0
    pick = lambda far, near: jnp.where(is_far, far[...], near[...]).reshape(near.shape[0] * planes, lanes)
    hb = jnp.concatenate([rows_of(r) for r in hb_refs], axis=0)
    slow = jnp.concatenate([rows_of(slow_ref)] + [pick(f, n) for f, n in zip(far_refs, near_refs)], axis=0)
    total = dot(m_ref[...], stacked(jnp.concatenate([hb, slow], axis=0)))
    tall = total[:rows] + dot(k_ref[...], stacked(pick(far_later, near_later)))
    later_ref[...] = base_ref[...] + tall.reshape(count, planes, lanes)
    block_ref[...] = total[rows:].reshape(block_ref.shape)


def final(kind, is_far, base, near_later, far_later, hb, slow_mine, near_slow, far_slow, mats):
    count, planes, length = base.shape
    own = slow_mine.shape[0]
    none = np.zeros((planes, planes), np.float32)
    k = thrice_constant(spread_variants([(plane_matrix(-planes),), (plane_matrix(planes),), (none,)], count))
    lanes = 2 * GROUP
    along = lambda n: pl.BlockSpec((n, planes, lanes), lambda i, kind, far: (0, 0, i))
    near = lambda n: pl.BlockSpec((n, planes, lanes), lambda i, kind, far: (0, 0, i * (1 - far[0])))
    far = lambda n: pl.BlockSpec((n, planes, lanes), lambda i, kind, far: (0, 0, i * far[0]))
    picked = pl.BlockSpec((pl.squeezed,) + k.shape[1:], lambda i, kind, far: (kind[0], 0, 0))
    return pl.pallas_call(
        functools.partial(final_kernel, len(hb)),
        grid_spec=pltpu.PrefetchScalarGridSpec(
            num_scalar_prefetch=2,
            grid=(length // lanes,),
            in_specs=[along(count), near(count), far(count)]
            + [along(own)] * (len(hb) + 1)
            + [near(own)] * len(near_slow)
            + [far(own)] * len(far_slow)
            + [picked, pl.BlockSpec(mats.shape, lambda i, kind, far: (0, 0))],
            out_specs=[along(count), along(own)],
        ),
        out_shape=[
            jax.ShapeDtypeStruct((count, planes, length), jnp.float32),
            jax.ShapeDtypeStruct((own, planes, length), jnp.float32),
        ],
        compiler_params=pltpu.CompilerParams(vmem_limit_bytes=VMEM),
        cost_estimate=pl.CostEstimate(flops=8_000_000_000, bytes_accessed=24 * base.size, transcendentals=0),
        name="final",
    )(kind, is_far, base, near_later, far_later, *hb, slow_mine, *near_slow, *far_slow, k, mats)


def after(x, *others):
    return lax.optimization_barrier((x,) + others)[0]


def local(blocks, later, potential):
    pair, own_rows, planes, length = blocks.shape
    count = later.shape[0]
    ns, nb = lax.axis_size("space"), lax.axis_size("band")
    s, band = lax.axis_index("space"), lax.axis_index("band")
    cells = planes * ns * length
    own = pair * own_rows
    both = ("space", "band")

    fast_pairs = [(i, i ^ 1) for i in range(ns)]
    near = [(i, i + 1) for i in range(1, ns - 1, 4)]
    near += [(j, i) for i, j in near]
    across = range(3, ns - 1, 4)
    far = [(i, i + 1) for i in across] + [(i + 1, i) for i in across]
    hop_one = [(i, i + 4) for i in across] + [(i + 1, i - 3) for i in across]
    hop_two = [(i + 4, i + 1) for i in across] + [(i - 3, i) for i in across]
    is_far = ((s % 4 == 3) & (s < ns - 1)) | ((s % 4 == 0) & (s > 0))
    two = is_far.astype(jnp.int32).reshape(1)
    ring = [(b + 1, b) for b in range(nb - 1)] + [(0, nb - 1)]

    odd = (s % 2).astype(jnp.int32).reshape(1)
    edge = (s == 0) | (s == ns - 1)
    kind = jnp.where(edge, 2, odd)
    before, behind = plane_matrix(-planes), plane_matrix(planes)
    slow_mat = jnp.where(edge, 0.0, jnp.where(s % 2 == 0, before, behind))

    mine = blocks.reshape(own, planes, length)
    slots, slow = [None] * nb, [None] * nb
    slots[0] = mine
    up = lambda x: lax.ppermute(x, "band", ring)
    down = lambda x: lax.ppermute(x, "band", [(j, i) for i, j in ring])
    swap = lambda x: lax.ppermute(x, "space", fast_pairs)
    near_ring = [(i * nb + b, i * nb + c) for i, _ in near for b, c in ring]
    near_up = lambda x: lax.ppermute(x, both, near_ring)
    near_down = lambda x: lax.ppermute(x, both, [(j, i) for i, j in near_ring])
    cross = lambda x: lax.ppermute(x, "space", far)

    middle = nb // 2
    order = [0] + sorted(range(1, nb), key=lambda k: (min(k, nb - k), k))
    slots[1], slots[-1] = up(mine), down(mine)
    fast_mine, fast_later = swap(mine), swap(later)
    hop = lax.ppermute(later, "space", hop_one)
    near_later = lax.ppermute(later, "space", near)
    slow_mine = lax.ppermute(mine, "space", near + far)
    hb = [None] * nb
    hb[0] = stencil(mine, fast_mine, odd, potential, own)
    base = stencil(later, fast_later, odd, potential, min(32, count))
    slots[1], slots[-1], hop, base, hb[0] = lax.optimization_barrier((slots[1], slots[-1], hop, base, hb[0]))
    for k in order[1:]:
        if slots[k] is None:
            slots[k] = up(slots[k - 1]) if k <= middle else down(slots[k + 1])
    far_later = lax.ppermute(hop, "space", hop_two)
    fast = {k: swap(slots[k]) for k in order[1:-1]}
    far_slow = {k: cross(slots[k]) for k in order[1:-1]}
    for k in order[1:-1]:
        hb[k] = stencil(slots[k], fast[k], odd, potential, own)
    known = gram([slots[k] for k in order[:-1]], after(later, *fast.values()))
    slots[middle], known, slow_mine, *rest = lax.optimization_barrier(
        (slots[middle], known, slow_mine, *[hb[k] for k in order[:-1]])
    )
    for k, h in zip(order[:-1], rest):
        hb[k] = h
    near_slow = {0: slow_mine}
    for k in order[1:-1]:
        near_slow[k] = near_up(near_slow[k - 1]) if k < middle else near_down(near_slow[(k + 1) % nb])
    far_slow[middle] = cross(slots[middle])
    copies = 4
    products = lax.all_gather(gram_last([slots[k] for k in order], later, known, copies), "space")
    hb[middle] = stencil(slots[middle], swap(slots[middle]), odd, potential, own)
    near_slow[middle] = near_up(near_slow[middle - 1])
    mats = mix(products, band, slow_mat, cells, nb, own_rows, count, order)
    pick = lambda d: [d[k] for k in order[1:]]
    h_later, h_block = final(
        kind, two, base, near_later, far_later, [hb[k] for k in order], slow_mine, pick(near_slow), pick(far_slow), mats
    )
    return h_block.reshape(blocks.shape), h_later


def solution(mesh):
    return jax.shard_map(
        local,
        mesh=mesh,
        in_specs=(P(None, "band", "space", None), P("band", "space", None), P("space", None)),
        out_specs=(P(None, "band", "space", None), P("band", "space", None)),
        check_vma=False,
    )
```

```python
import functools

import jax
import jax.numpy as jnp
import numpy as np
from jax import lax
from jax.experimental import pallas as pl
from jax.experimental.pallas import tpu as pltpu
from jax.sharding import PartitionSpec as P

NZ = 96
REACH = 4
LANE = 128
VMEM = 28 << 20

stencil_weights = (-205.0 / 72.0, 8.0 / 5.0, -1.0 / 5.0, 8.0 / 315.0, -1.0 / 560.0)
half_weights = tuple(-0.5 * w for w in stencil_weights)

GROUP = 4 * NZ
HIGHEST = lax.Precision.HIGHEST


def split(x):
    high = x.astype(jnp.bfloat16)
    low = (x - high.astype(jnp.float32)).astype(jnp.bfloat16)
    return high, low


def thrice(m):
    high, low = split(m)
    return jnp.concatenate([high, high, low], axis=1)


def stacked(x):
    high, low = split(x)
    return jnp.concatenate([high, low, high], axis=0)


def dot(a, b, dims=((1,), (0,))):
    return lax.dot_general(a, b, (dims, ((), ())), preferred_element_type=jnp.float32)


def exact(a, b, dims=((1,), (0,))):
    return lax.dot_general(a, b, (dims, ((), ())), precision=HIGHEST, preferred_element_type=jnp.float32)


def plane_matrix(offset):
    out = np.zeros((REACH, REACH), np.float32)
    for p in range(REACH):
        for q in range(REACH):
            shift = abs(q + offset - p)
            if 1 <= shift <= REACH:
                out[p, q] = half_weights[shift]
    return out


def spread_variants(left_of_variant, count):
    eye = np.eye(count, dtype=np.float32)
    return np.stack([np.concatenate([np.kron(eye, m) for m in ms], axis=1) for ms in left_of_variant])


def z_matrix():
    a = np.arange(GROUP)[:, None]
    o = np.arange(GROUP)[None, :]
    dz = np.abs(a - o)
    same = a // NZ == o // NZ
    out = np.zeros((GROUP, GROUP), np.float64)
    for step in range(1, REACH + 1):
        out += half_weights[step] * (same & (dz == step))
    out += 3.0 * half_weights[0] * (dz == 0)
    return out.astype(np.float32)


def thrice_constant(x):
    high = x.astype(jnp.bfloat16)
    low = (x - high.astype(np.float32)).astype(jnp.bfloat16)
    return jnp.asarray(np.concatenate([high, high, low], axis=-1))


def split_constant(x):
    high = x.astype(jnp.bfloat16)
    low = (x - high.astype(np.float32)).astype(jnp.bfloat16)
    return jnp.asarray(high), jnp.asarray(low)


def rows_of(ref):
    count, planes, lanes = ref.shape
    return ref[...].reshape(count * planes, lanes)


def one_hot(shape, row, column):
    r = lax.broadcasted_iota(jnp.int32, shape, 0)
    c = lax.broadcasted_iota(jnp.int32, shape, 1)
    return (row(r) == column(c)).astype(jnp.float32)


def gram_kernel(slots, *refs):
    b_refs, l_ref, out_ref, acc_ref = refs[:slots], refs[slots], refs[slots + 1], refs[slots + 2]
    step = pl.program_id(0)
    own, planes = b_refs[0].shape[:2]
    bh, bl = split(jnp.concatenate([rows_of(r) for r in b_refs], axis=0))
    lh, ll = split(rows_of(l_ref))
    rh = jnp.concatenate([bh, lh], axis=0)
    rl = jnp.concatenate([bl, ll], axis=0)
    part = dot(jnp.concatenate([bh, bh, bl], axis=1), jnp.concatenate([rh, rl, rh], axis=1), ((1,), (1,)))

    @pl.when(step == 0)
    def _():
        acc_ref[...] = part

    @pl.when(step > 0)
    def _():
        acc_ref[...] += part

    @pl.when(step == pl.num_programs(0) - 1)
    def _():
        full = acc_ref[...]
        m, n = full.shape
        full = full * one_hot((m, n), lambda r: r % planes, lambda c: c % planes)
        left = one_hot((m // planes, m), lambda r: r, lambda c: c // planes)
        place = lambda r: r // planes + jnp.where(r // planes < own * slots, 0, own)
        right = one_hot((n, out_ref.shape[1]), place, lambda c: c)
        out_ref[...] = exact(exact(left, full), right)


def gram(slots, later):
    own, planes, length = slots[0].shape
    rows = own * len(slots)
    count = later.shape[0]
    lanes = 2 * GROUP
    along = lambda n: pl.BlockSpec((n, planes, lanes), lambda i: (0, 0, i))
    return pl.pallas_call(
        functools.partial(gram_kernel, len(slots)),
        grid=(length // lanes,),
        in_specs=[along(own)] * len(slots) + [along(count)],
        out_specs=pl.BlockSpec((rows, rows + own + count), lambda i: (0, 0)),
        out_shape=jax.ShapeDtypeStruct((rows, rows + own + count), jnp.float32),
        scratch_shapes=[pltpu.VMEM((rows * planes, (rows + count) * planes), jnp.float32)],
        compiler_params=pltpu.CompilerParams(vmem_limit_bytes=VMEM),
        cost_estimate=pl.CostEstimate(
            flops=8_000_000_000, bytes_accessed=4 * (rows + count) * planes * length, transcendentals=0
        ),
        name="gram",
    )(*slots, later)


def gram_last_kernel(slots, *refs):
    b_refs, l_ref, known_ref, out_ref, acc_ref = refs[:slots], refs[slots], *refs[slots + 1 :]
    step = pl.program_id(0)
    own, planes = b_refs[0].shape[:2]
    size = own * planes
    rh, rl = split(jnp.concatenate([rows_of(r) for r in b_refs] + [rows_of(l_ref)], axis=0))
    here = slice(size * (slots - 1), size * slots)
    weights = jnp.concatenate([rh[here], rl[here]], axis=0)
    part = dot(jnp.concatenate([rh, rl], axis=0), weights, ((1,), (1,)))

    @pl.when(step == 0)
    def _():
        acc_ref[...] = part

    @pl.when(step > 0)
    def _():
        acc_ref[...] += part

    @pl.when(step == pl.num_programs(0) - 1)
    def _():
        n = rh.shape[0]
        full = acc_ref[...]
        full = full[:n] + full[n:]
        full = full * one_hot(full.shape, lambda r: r % planes, lambda c: c % planes)
        left = one_hot((own, full.shape[1]), lambda r: r, lambda c: (c % size) // planes)
        right = one_hot((n, n // planes), lambda r: r // planes, lambda c: c)
        new = exact(exact(left, full, ((1,), (1,))), right)
        rows = own * slots
        for copy in range(out_ref.shape[0] // rows):
            out_ref[copy * rows : (copy + 1) * rows - own, :] = known_ref[...]
            out_ref[(copy + 1) * rows - own : (copy + 1) * rows, :] = new


def gram_last(slots, later, known, copies):
    own, planes, length = slots[0].shape
    rows = own * len(slots)
    count = later.shape[0]
    lanes = 2 * GROUP
    along = lambda n: pl.BlockSpec((n, planes, lanes), lambda i: (0, 0, i))
    return pl.pallas_call(
        functools.partial(gram_last_kernel, len(slots)),
        grid=(length // lanes,),
        in_specs=[along(own)] * len(slots) + [along(count), pl.BlockSpec(known.shape, lambda i: (0, 0))],
        out_specs=pl.BlockSpec((copies * rows, rows + count), lambda i: (0, 0)),
        out_shape=jax.ShapeDtypeStruct((copies * rows, rows + count), jnp.float32),
        scratch_shapes=[pltpu.VMEM((2 * (rows + count) * planes, 2 * own * planes), jnp.float32)],
        compiler_params=pltpu.CompilerParams(vmem_limit_bytes=VMEM),
        cost_estimate=pl.CostEstimate(
            flops=4_000_000_000, bytes_accessed=4 * (rows + count) * planes * length, transcendentals=0
        ),
        name="gram_last",
    )(*slots, later, known)


def mix_kernel(band_ref, slow_ref, prod_ref, out_ref, *, cells, bands, own_rows, count, order):
    own = 2 * own_rows
    rows = bands * own
    block_rows = bands * own_rows
    planes = REACH
    band = band_ref[0]
    products = prod_ref[0, :rows, :]
    for d in range(1, prod_ref.shape[0]):
        products = products + prod_ref[d, :rows, :]
    products = products * (1.0 / cells)

    def home(r):
        turn, inside = r // own, r % own
        slot = jnp.zeros_like(r)
        for t, k in enumerate(order):
            slot = jnp.where(turn == t, k, slot)
        held = (slot + band) % bands
        return (inside // own_rows) * block_rows + held * own_rows + inside % own_rows

    place = one_hot((rows, rows), lambda r: r, home)
    last = rows - own
    flip = exact(products[last:, :last], one_hot((own, own), lambda r: r, lambda c: c), ((0,), (0,)))
    corr = jnp.concatenate(
        [jnp.concatenate([products[:last, :last], flip], axis=1), products[last:, :rows]], axis=0
    )
    corr = exact(exact(place, corr), place, ((1,), (1,)))
    eye = one_hot((rows, rows), lambda r: r, lambda c: c)
    table = jnp.concatenate([corr, eye, exact(place, products[:, rows:])], axis=1)
    tiles = [table[t : t + 8] for t in range(0, rows, 8)]
    row_id = lax.broadcasted_iota(jnp.int32, (8, 1), 0)
    for j in range(rows):
        t = j // 8
        pivot_row = tiles[t][j % 8 : j % 8 + 1]
        step = pivot_row * (1.0 / pivot_row[:, j : j + 1])
        tiles[t] = tiles[t] - jnp.where(row_id > j % 8, tiles[t][:, j : j + 1], 0.0) * step
        for u in range(t + 1, len(tiles)):
            tiles[u] = tiles[u] - tiles[u][:, j : j + 1] * step
    table = jnp.concatenate(tiles, axis=0)
    pivots = jnp.sum(table[:, :rows] * eye, axis=1, keepdims=True)
    scale = lax.rsqrt(pivots)
    scale = scale * (1.5 - 0.5 * pivots * scale * scale)
    inverse = table[:, rows : 2 * rows] * scale
    weights = table[:, 2 * rows :] * scale
    coefs = exact(weights, inverse, ((0,), (0,)))
    mine = one_hot((own, rows), lambda r: (r // own_rows) * block_rows + band * own_rows + r % own_rows, lambda c: c)
    mix = jnp.concatenate([-coefs, exact(mine, inverse)], axis=0)
    mix = exact(mix, place)
    outs = count + own
    tall = one_hot((outs * planes, outs), lambda r: r // planes, lambda c: c)
    wide = one_hot((rows, rows * planes), lambda r: r, lambda c: c // planes)
    spread = exact(exact(tall, mix), wide)
    p = lax.broadcasted_iota(jnp.int32, (8, spread.shape[1]), 0) % planes
    q = lax.broadcasted_iota(jnp.int32, (8, spread.shape[1]), 1) % planes
    pattern = jnp.zeros(p.shape, jnp.float32)
    for a in range(planes):
        for b in range(planes):
            pattern = jnp.where((p == a) & (q == b), slow_ref[a, b], pattern)
    same = (p == q).astype(jnp.float32)
    spread = spread.reshape(outs * planes // 8, 8, rows * planes)
    first = (spread * same[None]).reshape(outs * planes, rows * planes)
    second = (spread * pattern[None]).reshape(outs * planes, rows * planes)
    out_ref[...] = thrice(jnp.concatenate([first, second], axis=1))


def mix(products, band, slow_mat, cells, bands, own_rows, count, order):
    own = 2 * own_rows
    rows = bands * own
    planes = REACH
    return pl.pallas_call(
        functools.partial(mix_kernel, cells=cells, bands=bands, own_rows=own_rows, count=count, order=order),
        in_specs=[
            pl.BlockSpec(memory_space=pltpu.SMEM),
            pl.BlockSpec(memory_space=pltpu.SMEM),
            pl.BlockSpec(memory_space=pltpu.VMEM),
        ],
        out_specs=pl.BlockSpec(memory_space=pltpu.VMEM),
        out_shape=jax.ShapeDtypeStruct(((count + own) * planes, 6 * rows * planes), jnp.bfloat16),
        compiler_params=pltpu.CompilerParams(vmem_limit_bytes=VMEM),
        cost_estimate=pl.CostEstimate(flops=10_000_000_000, bytes_accessed=1 << 20, transcendentals=0),
        name="mix",
    )(band.reshape(1), slow_mat, products)


def along_y(vector, n, i, cache):
    rows = vector(i).shape[0]
    lane = lax.broadcasted_iota(jnp.int32, (rows, LANE), 1)

    def rolled(j, shift):
        if not 0 <= j < n:
            return jnp.zeros((rows, LANE), jnp.float32)
        if shift and (j, shift) not in cache:
            cache[j, shift] = pltpu.roll(vector(j), shift, 1)
        return cache[j, shift] if shift else vector(j)

    def joined(edge, j, k, shift):
        return jnp.where(lane < edge, rolled(j, shift), rolled(k, shift))

    one = joined(32, i, i + 1, 32) + joined(96, i - 1, i, 96)
    two = joined(64, i + 1, i + 2, 64) + joined(64, i - 2, i - 1, 64)
    three = joined(96, i + 2, i + 3, 96) + joined(32, i - 3, i - 2, 32)
    four = rolled(i + 3, 0) + rolled(i - 3, 0)
    return half_weights[1] * one + half_weights[2] * two + half_weights[3] * three + half_weights[4] * four


def stencil_kernel(x_ref, halo_ref, m_ref, z_ref, v_ref, out_ref):
    count, planes, length = x_ref.shape
    rows = count * planes
    x_all = rows_of(x_ref)
    cache = {}
    vector = lambda i: x_all[:, i * LANE : (i + 1) * LANE]
    for g in range(length // GROUP):
        here = slice(g * GROUP, (g + 1) * GROUP)
        x = x_all[:, here]
        xh, xl = split(x)
        total = dot(jnp.concatenate([xh, xl, xh], axis=1), z_ref[...])
        total += dot(m_ref[...], stacked(jnp.concatenate([x, halo_ref[:, :, here].reshape(rows, GROUP)], axis=0)))
        each = GROUP // LANE
        total += jnp.concatenate([along_y(vector, length // LANE, g * each + i, cache) for i in range(each)], axis=1)
        weighted = v_ref[:, here][None] * x.reshape(rows // 8, 8, GROUP)
        out_ref[:, :, here] = (total + weighted.reshape(rows, GROUP)).reshape(count, planes, GROUP)


def stencil(x, halo, odd, potential, block):
    count, planes, length = x.shape
    size = block * planes
    within = plane_matrix(0)
    m = thrice_constant(spread_variants([(within, plane_matrix(planes)), (within, plane_matrix(-planes))], block))
    zh, zl = split_constant(z_matrix())
    z = jnp.concatenate([zh, zh, zl], axis=0)
    v = jnp.concatenate([potential, potential], axis=0)
    spec = pl.BlockSpec((block, planes, length), lambda i, odd: (i, 0, 0))
    picked = pl.BlockSpec((pl.squeezed,) + m.shape[1:], lambda i, odd: (odd[0], 0, 0))
    fixed = lambda a: pl.BlockSpec(a.shape, lambda i, odd: (0, 0))
    return pl.pallas_call(
        lambda odd_ref, *refs: stencil_kernel(*refs),
        grid_spec=pltpu.PrefetchScalarGridSpec(
            num_scalar_prefetch=1,
            grid=(count // block,),
            in_specs=[spec, spec, picked, fixed(z), fixed(v)],
            out_specs=spec,
        ),
        out_shape=jax.ShapeDtypeStruct(x.shape, jnp.float32),
        compiler_params=pltpu.CompilerParams(vmem_limit_bytes=VMEM),
        cost_estimate=pl.CostEstimate(flops=100_000_000 * count, bytes_accessed=12 * x.size, transcendentals=0),
        name="stencil",
    )(odd, x, halo, m, z, v)


def final_kernel(slots, kind_ref, far_ref, base_ref, near_later, far_later, *refs):
    hb_refs, refs = refs[:slots], refs[slots:]
    slow_ref, near_refs, far_refs = refs[0], refs[1:slots], refs[slots : 2 * slots - 1]
    k_ref, m_ref, later_ref, block_ref = refs[2 * slots - 1 :]
    count, planes, lanes = base_ref.shape
    rows = count * planes
    is_far = far_ref[0] > 0
    pick = lambda far, near: jnp.where(is_far, far[...], near[...]).reshape(near.shape[0] * planes, lanes)
    hb = jnp.concatenate([rows_of(r) for r in hb_refs], axis=0)
    slow = jnp.concatenate([rows_of(slow_ref)] + [pick(f, n) for f, n in zip(far_refs, near_refs)], axis=0)
    total = dot(m_ref[...], stacked(jnp.concatenate([hb, slow], axis=0)))
    tall = total[:rows] + dot(k_ref[...], stacked(pick(far_later, near_later)))
    later_ref[...] = base_ref[...] + tall.reshape(count, planes, lanes)
    block_ref[...] = total[rows:].reshape(block_ref.shape)


def final(kind, is_far, base, near_later, far_later, hb, slow_mine, near_slow, far_slow, mats):
    count, planes, length = base.shape
    own = slow_mine.shape[0]
    none = np.zeros((planes, planes), np.float32)
    k = thrice_constant(spread_variants([(plane_matrix(-planes),), (plane_matrix(planes),), (none,)], count))
    lanes = 2 * GROUP
    along = lambda n: pl.BlockSpec((n, planes, lanes), lambda i, kind, far: (0, 0, i))
    near = lambda n: pl.BlockSpec((n, planes, lanes), lambda i, kind, far: (0, 0, i * (1 - far[0])))
    far = lambda n: pl.BlockSpec((n, planes, lanes), lambda i, kind, far: (0, 0, i * far[0]))
    picked = pl.BlockSpec((pl.squeezed,) + k.shape[1:], lambda i, kind, far: (kind[0], 0, 0))
    return pl.pallas_call(
        functools.partial(final_kernel, len(hb)),
        grid_spec=pltpu.PrefetchScalarGridSpec(
            num_scalar_prefetch=2,
            grid=(length // lanes,),
            in_specs=[along(count), near(count), far(count)]
            + [along(own)] * (len(hb) + 1)
            + [near(own)] * len(near_slow)
            + [far(own)] * len(far_slow)
            + [picked, pl.BlockSpec(mats.shape, lambda i, kind, far: (0, 0))],
            out_specs=[along(count), along(own)],
        ),
        out_shape=[
            jax.ShapeDtypeStruct((count, planes, length), jnp.float32),
            jax.ShapeDtypeStruct((own, planes, length), jnp.float32),
        ],
        compiler_params=pltpu.CompilerParams(vmem_limit_bytes=VMEM),
        cost_estimate=pl.CostEstimate(flops=8_000_000_000, bytes_accessed=24 * base.size, transcendentals=0),
        name="final",
    )(kind, is_far, base, near_later, far_later, *hb, slow_mine, *near_slow, *far_slow, k, mats)


def after(x, *others):
    return lax.optimization_barrier((x,) + others)[0]


def local(blocks, later, potential):
    pair, own_rows, planes, length = blocks.shape
    count = later.shape[0]
    ns, nb = lax.axis_size("space"), lax.axis_size("band")
    s, band = lax.axis_index("space"), lax.axis_index("band")
    cells = planes * ns * length
    own = pair * own_rows
    both = ("space", "band")

    fast_pairs = [(i, i ^ 1) for i in range(ns)]
    near = [(i, i + 1) for i in range(1, ns - 1, 4)]
    near += [(j, i) for i, j in near]
    across = range(3, ns - 1, 4)
    far = [(i, i + 1) for i in across] + [(i + 1, i) for i in across]
    hop_one = [(i, i + 4) for i in across] + [(i + 1, i - 3) for i in across]
    hop_two = [(i + 4, i + 1) for i in across] + [(i - 3, i) for i in across]
    is_far = ((s % 4 == 3) & (s < ns - 1)) | ((s % 4 == 0) & (s > 0))
    two = is_far.astype(jnp.int32).reshape(1)
    ring = [(b + 1, b) for b in range(nb - 1)] + [(0, nb - 1)]

    odd = (s % 2).astype(jnp.int32).reshape(1)
    edge = (s == 0) | (s == ns - 1)
    kind = jnp.where(edge, 2, odd)
    before, behind = plane_matrix(-planes), plane_matrix(planes)
    slow_mat = jnp.where(edge, 0.0, jnp.where(s % 2 == 0, before, behind))

    mine = blocks.reshape(own, planes, length)
    slots, slow = [None] * nb, [None] * nb
    slots[0] = mine
    up = lambda x: lax.ppermute(x, "band", ring)
    down = lambda x: lax.ppermute(x, "band", [(j, i) for i, j in ring])
    swap = lambda x: lax.ppermute(x, "space", fast_pairs)
    near_ring = [(i * nb + b, i * nb + c) for i, _ in near for b, c in ring]
    near_up = lambda x: lax.ppermute(x, both, near_ring)
    near_down = lambda x: lax.ppermute(x, both, [(j, i) for i, j in near_ring])
    cross = lambda x: lax.ppermute(x, "space", far)

    middle = nb // 2
    order = [0] + sorted(range(1, nb), key=lambda k: (min(k, nb - k), k))
    slots[1], slots[-1] = up(mine), down(mine)
    fast_mine, fast_later = swap(mine), swap(later)
    hop = lax.ppermute(later, "space", hop_one)
    near_later = lax.ppermute(later, "space", near)
    slow_mine = lax.ppermute(mine, "space", near + far)
    hb = [None] * nb
    hb[0] = stencil(mine, fast_mine, odd, potential, own)
    base = stencil(later, fast_later, odd, potential, min(32, count))
    for k in order[1:]:
        if slots[k] is None:
            slots[k] = up(after(slots[k - 1], base)) if k <= middle else down(after(slots[k + 1], base))
    slots[1], slots[-1], hop, base, hb[0] = lax.optimization_barrier((slots[1], slots[-1], hop, base, hb[0]))
    far_later = lax.ppermute(hop, "space", hop_two)
    fast = {k: swap(slots[k]) for k in order[1:-1]}
    far_slow = {k: cross(slots[k]) for k in order[1:-1]}
    for k in order[1:-1]:
        hb[k] = stencil(slots[k], fast[k], odd, potential, own)
    known = gram([slots[k] for k in order[:-1]], after(later, *fast.values()))
    slots[middle], known, slow_mine, near_later, *rest = lax.optimization_barrier(
        (slots[middle], known, slow_mine, near_later, *[hb[k] for k in order[:-1]])
    )
    for k, h in zip(order[:-1], rest):
        hb[k] = h
    near_slow = {0: slow_mine}
    for k in order[1:-1]:
        near_slow[k] = near_up(near_slow[k - 1]) if k < middle else near_down(near_slow[(k + 1) % nb])
    far_slow[middle] = cross(slots[middle])
    copies = 4
    products = lax.all_gather(gram_last([slots[k] for k in order], later, known, copies), "space")
    hb[middle] = stencil(slots[middle], swap(slots[middle]), odd, potential, own)
    near_slow[middle] = near_up(near_slow[middle - 1])
    mats = mix(products, band, slow_mat, cells, nb, own_rows, count, order)
    pick = lambda d: [d[k] for k in order[1:]]
    h_later, h_block = final(
        kind, two, base, near_later, far_later, [hb[k] for k in order], slow_mine, pick(near_slow), pick(far_slow), mats
    )
    return h_block.reshape(blocks.shape), h_later


def solution(mesh):
    return jax.shard_map(
        local,
        mesh=mesh,
        in_specs=(P(None, "band", "space", None), P("band", "space", None), P("space", None)),
        out_specs=(P(None, "band", "space", None), P("band", "space", None)),
        check_vma=False,
    )
```
